256 devices in a mesh: tm: 64 (over z, y, core), col: 4 (over x).
Axes of the slice: x: 4, y: 4, z: 8, core: 2. Of those that a mesh axis runs over, the one named last changes fastest.
Arguments:
- precision_blocks: bfloat16 [128, 1024, 1024], P('tm', None, 'col'), may hold values from -1 to 1
- coupling: bfloat16 [128, 1024, 1024], P('tm', 'col'), may hold values from -2 to 2
- arrow_rows: bfloat16 [128, 16, 1024], P('tm'), may hold values from -0.1875 to 0.1875
- corner_base: float32 [16, 16], replicated, may hold values from -6 to 6
Outputs:
- sigma_blocks: bfloat16 [128, 1024, 1024], P('tm', None, 'col')
- arrow_block: bfloat16 [128, 16, 1024], P('tm', None, 'col')
- corner: float32 [16, 16], replicated
The draws below stay inside these ranges and needn't reach their ends.
All inputs are finite; a program needn't handle non-finite values.
Results may differ from the reference program's by a relative error of at most 0.023.
The reference program's roundings to bfloat16 on the way count: a program that leaves them out, or rounds other values in their place, can miss the bound.
Values may be sent and summed in bfloat16 or wider, within the bound.
A program may use at most 64 MiB of HBM per device.

```python
import jax
import jax.numpy as jnp

B = 1024
AR = 16
EPOCH_COUNT = 128


def laggard_sample(key):
    half_sample = jax.random.uniform(jax.random.fold_in(key, 5), (B // 2,))
    return jnp.concatenate([half_sample, half_sample], 0)


def draw_coupling(key, part):
    picking_sample = laggard_sample(key)
    key = jax.random.fold_in(key, 11)
    descendant_seeds = jax.random.split(key, 4)
    laggard_portion = 0.5
    laggard_throughput = jnp.sqrt(1.0 - 1.5 / EPOCH_COUNT)
    rapid_throughput = jax.random.uniform(descendant_seeds[1], (EPOCH_COUNT, B), minval=0.15, maxval=0.6)
    arrival_bunches = jnp.where(jax.random.uniform(descendant_seeds[2], (EPOCH_COUNT, 1)) < 3.0 / EPOCH_COUNT, jnp.sqrt(0.6), 1.0)
    link_throughput = jnp.where(picking_sample[None, :] < laggard_portion, laggard_throughput * arrival_bunches, rapid_throughput)
    crossing = jnp.roll(jnp.eye(B, dtype=jnp.float32), B // 2, axis=0)
    mixing = jax.random.normal(descendant_seeds[3], (EPOCH_COUNT, B, B), jnp.float32) * (0.2 / jnp.sqrt(B * 1.0))
    return (mixing + crossing[None, :, :] * link_throughput[:, None, :]).astype(jnp.bfloat16)


def draw_precision_blocks(key, part):
    picking_sample = laggard_sample(key)
    key = jax.random.fold_in(key, 23)
    descendant_seeds = jax.random.split(key, 3)
    lower, upper, spread, laggard_portion = (0.05, 0.5, 0.07, 0.5)
    raw = jax.random.normal(descendant_seeds[0], (EPOCH_COUNT, B, B), jnp.float32) * (spread / jnp.sqrt(B * 1.0))
    symmetric = raw + jnp.swapaxes(raw, 1, 2)
    diag_values = jnp.exp(jax.random.uniform(descendant_seeds[1], (EPOCH_COUNT, B), minval=jnp.log(lower), maxval=jnp.log(upper)))
    laggard = picking_sample[None, :] < laggard_portion
    terminal_values = jax.random.uniform(descendant_seeds[2], (EPOCH_COUNT, B), minval=0.3, maxval=0.9)
    steps_index = jnp.arange(EPOCH_COUNT)[:, None]
    middle_values = jnp.where(laggard, diag_values * (3.0 / EPOCH_COUNT), diag_values)
    diag_final = jnp.where(laggard & (steps_index >= EPOCH_COUNT - 2), terminal_values, middle_values)
    identity = jnp.eye(B, dtype=jnp.float32)
    return (symmetric + identity[None, :, :] * diag_final[:, None, :]).astype(jnp.bfloat16)


def block_levels(rng, dims, cuts, smallest, top_value):
    def one(dim, shards_of):
        steps = jax.random.uniform(jax.random.fold_in(jax.random.fold_in(rng, 6), dim), (shards_of,), jnp.float32, smallest / len(cuts), top_value / len(cuts))
        return jnp.repeat(jnp.exp(steps), dims[dim] // shards_of).reshape((-1,) + (1,) * (len(dims) - dim - 1))

    level = one(*cuts[0])
    for cut in cuts[1:]:
        level = level * one(*cut)
    return level


def scatter_about(own_key, shape, deviation, bound, cuts=(), kind=jnp.bfloat16):
    entries = jax.random.normal(own_key, shape, jnp.float32) * deviation
    if len(cuts) > 0:
        entries = block_levels(own_key, shape, cuts, -0.22, 0.18) * entries
    return jnp.clip(entries, min=-bound, max=bound).astype(kind)


def setup_inputs(seed: int = 0) -> dict:
    streams_of = jax.random.split(jax.random.key(seed), 5)
    precision_blocks = draw_precision_blocks(jax.random.fold_in(streams_of[4], 71), 0)
    coupling = draw_coupling(jax.random.fold_in(streams_of[4], 71), 0)
    arrow_rows = scatter_about(streams_of[2], (EPOCH_COUNT, AR, B), B ** -0.5, 0.1875, ((0, 64),))
    corner_base = scatter_about(streams_of[3], (AR, AR), 1.0, 6.0, (), jnp.float32)
    return dict(precision_blocks=precision_blocks, coupling=coupling, arrow_rows=arrow_rows, corner_base=corner_base)


def batched_product(left, right):
    return jnp.einsum("pij,pjk->pik", left.astype(jnp.float32), right.astype(jnp.float32))


def transposed_product(left, right):
    return jnp.einsum("pji,pjk->pik", left.astype(jnp.float32), right.astype(jnp.float32))


def reference(precision_blocks, coupling, arrow_rows, corner_base):
    d_first = precision_blocks[0::2]
    d_second = precision_blocks[1::2]
    g_first = coupling[0::2]
    g_second = coupling[1::2]
    state_h = batched_product(g_second, g_first).astype(jnp.bfloat16)
    product = batched_product(d_second, g_first).astype(jnp.bfloat16)
    state_s = (d_first.astype(jnp.float32) + transposed_product(g_first, product)).astype(jnp.bfloat16)
    partitions = state_s.shape[0]
    sections = partitions.bit_length() - 1
    for section_index in range(sections):
        distance = 1 << section_index
        padding = jnp.zeros((distance,) + state_s.shape[1:], state_s.dtype)
        later_s = jnp.concatenate([state_s[distance:], padding], 0)
        later_h = jnp.concatenate([state_h[distance:], padding], 0)
        product = batched_product(later_s, state_h).astype(jnp.bfloat16)
        new_s = (state_s.astype(jnp.float32) + transposed_product(state_h, product)).astype(jnp.bfloat16)
        if section_index + 1 < sections:
            state_h = batched_product(later_h, state_h).astype(jnp.bfloat16)
        state_s = new_s
    padding = jnp.zeros((1,) + state_s.shape[1:], state_s.dtype)
    next_s = jnp.concatenate([state_s[1:], padding], 0)
    product = batched_product(next_s, g_second).astype(jnp.bfloat16)
    sigma_odd = (d_second.astype(jnp.float32) + transposed_product(g_second, product)).astype(jnp.bfloat16)
    sigma_blocks = jnp.stack([state_s, sigma_odd], 1).reshape(precision_blocks.shape)
    arrow_full = jnp.einsum("tai,tij->taj", arrow_rows.astype(jnp.float32), sigma_blocks.astype(jnp.float32))
    corner_term = jnp.einsum("taj,tbj->ab", arrow_full, arrow_rows.astype(jnp.float32))
    corner = corner_base + corner_term / EPOCH_COUNT
    return sigma_blocks, arrow_full.astype(jnp.bfloat16), corner
```

```python
import functools

import jax
import jax.numpy as jnp
from jax import lax
from jax.experimental import pallas as pl
from jax.experimental.pallas import tpu as pltpu
from jax.sharding import PartitionSpec as P

MESH = pl.DeviceIdType.MESH
BF16 = jnp.bfloat16
F32 = jnp.float32
X = 4
SENDS = 420
RECVS = 420


def dot(a, b):
    return jnp.dot(a, b, preferred_element_type=F32)


class Links:
    def __init__(self, send, recv):
        self.send, self.recv = send, recv
        self.sends = self.recvs = 0
        self.pending = []

    def take_recv(self, count=1):
        base = self.recvs
        self.recvs += count
        assert self.recvs <= RECVS
        return base

    def take_send(self):
        self.sends += 1
        assert self.sends <= SENDS
        return self.sends - 1

    def copy(self, src, dst, slot, tm, col, when=None):
        sem = self.send.at[self.take_send()]

        def start():
            pltpu.make_async_remote_copy(
                src_ref=src, dst_ref=dst, send_sem=sem, recv_sem=self.recv.at[slot],
                device_id=(tm, col), device_id_type=MESH).start()

        def finish():
            pltpu.make_async_copy(src, src, sem).wait()

        if when is None:
            start()
            self.pending.append(finish)
        else:
            pl.when(when)(start)
            self.pending.append(lambda: pl.when(when)(finish))

    def copy_or_keep(self, src, dst, slot, tm, col, here, when=None):
        there = jnp.logical_not(here)
        if when is not None:
            here, there = jnp.logical_and(when, here), jnp.logical_and(when, there)

        @pl.when(here)
        def _():
            pltpu.make_async_copy(src, dst, self.recv.at[slot]).start()

        self.copy(src, dst, slot, tm, col, there)

    def wait(self, dst, slot):
        pltpu.make_async_copy(dst, dst, self.recv.at[slot]).wait()

    def drain(self):
        for finish in self.pending:
            finish()


def kernel(groups, D, G, R, cb, sig, arrow, corner,
           GF, HF, LA, LH, T, PT, A, B, BT, DB, DT, DS, OT, ON, OS, C1, C2, C3, send, recv):
    n, w = D.shape[1], D.shape[2]
    h, hw = n // 2, w // 2
    levels = groups.bit_length() - 1
    gy = min(4, groups)
    gz = groups // gy
    tm, x = lax.axis_index("tm"), lax.axis_index("col")
    i = lax.rem(tm, 2)
    q = tm // 2
    sib = 2 * q + 1 - i
    head = x // 2
    links = Links(send, recv)
    around = [lax.rem(x + d, X) for d in range(X)]
    right, left = around[1], around[3]

    def group_at(offset):
        return lax.rem(q + (offset + groups) % groups, groups)

    partners = [(sib, x)]
    for d in (1, 2, 3):
        partners += [(2 * q + c, around[d]) for c in (0, 1)]
    offsets = set()
    for k in range(levels):
        offsets |= {(1 << k) % groups, (-(1 << k)) % groups}
    partners += [(2 * group_at(o) + i, x) for o in sorted(offsets)]
    qy, qz = lax.rem(q, gy), q // gy
    ys = [(qz * gy + lax.rem(qy + d, gy)) for d in range(1, gy)]
    zs = [(lax.rem(qz + d, gz) * gy + qy) for d in range(1, gz)]
    partners += [(2 * g + i, x) for g in ys + zs]
    barrier = pltpu.get_barrier_semaphore()
    for partner in partners:
        pl.semaphore_signal(barrier, inc=1, device_id=partner, device_id_type=MESH)
    pl.semaphore_wait(barrier, len(partners))

    def rows_of(chip):
        return pl.ds(pl.multiple_of(chip * w, w), w)

    mine = rows_of(x)
    my_half = pl.ds(pl.multiple_of(i * h, h), h)
    its_half = pl.ds(pl.multiple_of((1 - i) * h, h), h)

    def top(chip):
        return pl.ds(pl.multiple_of(chip * w, w), hw)

    def bottom(chip):
        return pl.ds(pl.multiple_of(chip * w + hw, hw), hw)

    class Gather:
        def __init__(self, buf):
            self.buf, self.slot = buf, links.take_recv(6)

        def start(self):
            b, s = self.buf, self.slot
            links.copy(b.at[top(x)], b.at[top(x)], s, tm, right)
            links.copy(b.at[bottom(x)], b.at[bottom(x)], s + 3, tm, left)
            links.copy(b.at[bottom(x)], b.at[bottom(x)], s + 1, tm, right)
            links.copy(b.at[top(x)], b.at[top(x)], s + 2, tm, left)
            return self

        def mid(self):
            b, s = self.buf, self.slot
            links.wait(b.at[top(left)], s)
            links.copy(b.at[top(left)], b.at[top(left)], s + 4, tm, right)
            links.wait(b.at[bottom(right)], s + 3)
            links.copy(b.at[bottom(right)], b.at[bottom(right)], s + 5, tm, left)

        def end(self):
            b, s = self.buf, self.slot
            links.wait(b.at[bottom(left)], s + 1)
            links.wait(b.at[top(right)], s + 2)
            links.wait(b.at[top(around[2])], s + 4)
            links.wait(b.at[bottom(around[2])], s + 5)

    def exchange_start(buf, value):
        slot = links.take_recv()
        buf[i] = value
        links.copy(buf.at[i], buf.at[i], slot, sib, x)
        return lambda: links.wait(buf.at[1 - i], slot)

    class Turn:
        def __init__(self, index):
            self.buf, self.far, self.near = T.at[index], links.take_recv(4), links.take_recv(4)

        def receive(self, own):
            buf = self.buf
            for d in (1, 3, 2):
                s = around[d]
                links.wait(buf.at[s, i], self.far + s)
                links.copy(buf.at[s, i], buf.at[s, i], self.near + s, sib, x)

            @pl.when(jnp.logical_not(own))
            def _():
                links.wait(buf.at[x], self.near + x)

            for d in (1, 3, 2):
                s = around[d]
                links.wait(buf.at[s, 1 - i], self.near + s)

    turns = [0]

    def turn_start(value):
        index = turns[0]
        turns[0] += 1
        turn = Turn(index)
        value = value.astype(BF16)
        own = i == head
        for j in (0, 1):
            PT[index, j] = value[:, j * w:(j + 1) * w].T.reshape(2, hw, w)
        for j in (1, 0):
            chip = 2 * i + j
            for c in (0, 1):
                links.copy(PT.at[index, j, c], turn.buf.at[x, c], turn.far + x,
                           2 * q + c, chip, chip != x)

        @pl.when(own)
        def _():
            turn.buf[x] = PT[index, lax.rem(x, 2)]

        links.copy(PT.at[index, lax.rem(x, 2)], turn.buf.at[x], turn.near + x, sib, x, own)
        return lambda: turn.receive(own)

    def times_halves(L, H):
        return dot(L[0], H[0:h]) + dot(L[1], H[h:n])

    def times_blocks(Tb, H):
        out = dot(Tb[0].reshape(w, w), H[0:w])
        for k in range(1, X):
            out += dot(Tb[k].reshape(w, w), H[k * w:(k + 1) * w])
        return out

    def add_blocks(own, U):
        return jnp.concatenate(
            [own[0].astype(F32) + U[:, :w], own[1].astype(F32) + U[:, w:]], axis=1).astype(BF16)

    def keep_start(stage, buf, value):
        slot = links.take_recv(2)
        for j in (0, 1):
            stage[j] = value[:, j * w:(j + 1) * w].T
        for j in (1, 0):
            links.copy_or_keep(stage.at[j], buf.at[lax.rem(x, 2)], slot + lax.rem(x, 2),
                               2 * q + head, 2 * i + j,
                               jnp.logical_and(2 * i + j == x, head == i))

        def receive():
            for b in (0, 1):
                links.wait(buf.at[b], slot + b)
        return receive

    def spread_start(s, buf, core):
        slot = links.take_recv(2)
        sender = i == core
        for d in (1, 3, 2, 0):
            chip = around[d]
            links.copy_or_keep(D.at[s, rows_of(chip)], buf.at[lax.rem(x, 2)],
                               slot + lax.rem(x, 2), 2 * q + head, chip,
                               jnp.logical_and(d == 0, head == i), sender)

        def receive():
            for b in (0, 1):
                links.wait(buf.at[b], slot + b)
        return receive

    g_near = links.take_recv(2)
    for s in (1 - i, i):
        links.copy(G.at[s, :, its_half], GF.at[2 * i + s, mine], g_near + s, sib, x)

    rows3 = Turn(turns[0])
    turns[0] += 1
    for d in (1, 3, 2):
        chip = around[d]
        for c in (0, 1):
            at = pl.ds(pl.multiple_of(chip * w + c * hw, hw), hw)
            links.copy(D.at[1, at], rows3.buf.at[x, c], rows3.far + x, 2 * q + c, chip, i == 1)
    at = pl.multiple_of(x * w, w)
    DS[...] = D[1, pl.ds(at, w)].reshape(2, hw, w)

    @pl.when(i == 1)
    def _():
        rows3.buf[x] = DS[...]

    links.copy(DS, rows3.buf.at[x], rows3.near + x, sib, x, i == 1)

    for s in (0, 1):
        GF[2 * i + s, mine] = G[s, :, my_half]
    links.wait(GF.at[2 * (1 - i) + i, mine], g_near + i)
    gather2 = Gather(GF.at[2]).start()
    gather1 = Gather(GF.at[1])
    gather0 = Gather(GF.at[0])
    gather3 = Gather(GF.at[3])

    d_near = links.take_recv(2)
    for s in (0, 1):
        OT[s] = D[s, its_half].T
        links.copy(OT.at[s], DT.at[2 * i + s], d_near + s, sib, x)
        DT[2 * i + s] = D[s, my_half].T

    rows3.receive(i == 1)
    got_d1 = spread_start(1, DB.at[0], 0)
    links.wait(GF.at[2 * (1 - i) + 1 - i, mine], g_near + 1 - i)
    x0 = exchange_start(LH.at[0], GF[3, mine])
    gather2.mid()
    gather1.start()
    gather2.end()
    product = times_blocks(rows3.buf, GF.at[2])
    turn = turn_start(product)
    x0()
    x1 = exchange_start(LH.at[1], times_halves(LH.at[0], GF.at[2]).astype(BF16))
    for s in (0, 1):
        links.wait(DT.at[2 * (1 - i) + s], d_near + s)
    gather1.mid()
    turn()
    state = (times_blocks(T.at[1], GF.at[2]) + DT[2].astype(F32)).astype(BF16)
    a1 = exchange_start(LA.at[0], state)
    gather0.start()
    gather1.end()
    x1()
    x2 = exchange_start(LH.at[2], times_halves(LH.at[1], GF.at[1]).astype(BF16))
    a1()
    turn = turn_start(times_halves(LA.at[0], GF.at[1]))
    gather0.mid()
    got_d1()
    turn()
    state = add_blocks(DB.at[0], times_blocks(T.at[2], GF.at[1]))
    a2 = exchange_start(LA.at[1], state)
    gather0.end()
    x2()
    HF[0, mine] = times_halves(LH.at[2], GF.at[0]).astype(BF16)
    a2()
    turn = turn_start(times_halves(LA.at[1], GF.at[0]))
    gather = Gather(HF.at[0]).start()

    def later_start(src, buf, e, keep, want):
        slot, near = links.take_recv(2), links.take_recv(2)
        for c in (0, 1):
            at = pl.ds(c * hw, hw)
            links.copy(src.at[at], buf.at[i, at], slot + c, 2 * group_at(-e) + i, x, keep)

        def receive():
            for c in (0, 1):
                at = pl.ds(c * hw, hw)

                @pl.when(want)
                def _():
                    links.wait(buf.at[i, at], slot + c)

                links.copy(buf.at[i, at], buf.at[i, at], near + c, sib, x, want)

            @pl.when(want)
            def _():
                for c in (0, 1):
                    links.wait(buf.at[1 - i, pl.ds(c * hw, hw)], near + c)

            @pl.when(jnp.logical_not(want))
            def _():
                buf[...] = jnp.zeros_like(buf)
        return receive

    def send_state(src, buf, e):
        return later_start(src, buf, e, q >= e, q + e < groups)

    def send_map(src, buf, e):
        return later_start(src, buf, e, jnp.logical_and(q >= e, q + e < groups),
                           q + 2 * e < groups)

    got_h = send_map(HF.at[0, mine], LH.at[3], 1) if levels > 1 else None
    gather.mid()
    turn()
    A[0] = (times_blocks(T.at[3], GF.at[0]) + DT[0].astype(F32)).astype(BF16)
    got_a = send_state(A.at[0], LA.at[2], 1)
    got_b = keep_start(BT.at[0], B.at[0], A[0])
    got_d2 = None
    for k in range(levels):
        final = k + 1 == levels
        e = 1 << k
        gather.end()
        if not final:
            got_h()
            HF[k + 1, mine] = times_halves(LH.at[3 + k], HF.at[k]).astype(BF16)
            gather = Gather(HF.at[k + 1]).start()
            if k + 2 < levels:
                got_h = send_map(HF.at[k + 1, mine], LH.at[4 + k], 2 * e)
        else:
            gather3.start()
            gather = gather3
            got_d2 = spread_start(0, DB.at[1], 1)
        got_a()
        turn = turn_start(times_halves(LA.at[2 + k], HF.at[k]))
        gather.mid()
        got_b()
        turn()
        A[k + 1] = add_blocks(B.at[k], times_blocks(T.at[4 + k], HF.at[k]))
        if not final:
            got_a = send_state(A.at[k + 1], LA.at[3 + k], 2 * e)
            got_b = keep_start(BT.at[k + 1], B.at[k + 1], A[k + 1])

    def out_rows_start(index, value, core):
        slot = links.take_recv(X)
        for j in (0, 1):
            ON[index, j] = value[:, j * w:(j + 1) * w]
        for j in (1, 0):
            chip = 2 * i + j
            links.copy_or_keep(ON.at[index, j], sig.at[0, mine], slot + x, 2 * q + core, chip,
                               jnp.logical_and(chip == x, i == core))

        def receive():
            @pl.when(i == core)
            def _():
                for chip in range(X):
                    links.wait(sig.at[0, pl.ds(chip * w, w)], slot + chip)
        return receive

    def out_turned_start(index, value, core):
        slot = links.take_recv(2)
        OS[index] = value.T
        links.copy_or_keep(OS.at[index], sig.at[1, my_half], slot + i, 2 * q + core, x, i == core)

        def receive():
            @pl.when(i == core)
            def _():
                for c in (0, 1):
                    links.wait(sig.at[1, pl.ds(c * h, h)], slot + c)
        return receive

    base = 2 + levels
    got_a = send_state(A.at[levels], LA.at[base], 1)
    out0 = out_rows_start(0, A[levels], 0)
    gather3.end()
    got_a()
    turn = turn_start(times_halves(LA.at[base], GF.at[3]))
    turn()
    state = (times_blocks(T.at[4 + levels], GF.at[3]) + DT[3].astype(F32)).astype(BF16)
    a3 = exchange_start(LA.at[base + 1], state)
    out3 = out_turned_start(0, state, 1)
    a3()
    turn = turn_start(times_halves(LA.at[base + 1], GF.at[2]))
    got_d2()
    turn()
    state = add_blocks(DB.at[1], times_blocks(T.at[5 + levels], GF.at[2]))
    a4 = exchange_start(LA.at[base + 2], state)
    out2 = out_rows_start(1, state, 1)
    a4()
    turn = turn_start(times_halves(LA.at[base + 2], GF.at[1]))
    out0()
    out3()
    out2()
    turn()
    state = (times_blocks(T.at[6 + levels], GF.at[1]) + DT[1].astype(F32)).astype(BF16)
    out1 = out_turned_start(1, state, 0)

    out1()
    total = jnp.zeros((R.shape[1], R.shape[1]), F32)
    for s in (0, 1):
        full = dot(R[s], sig[s])
        arrow[s] = full.astype(BF16)
        panel = R[s, :, pl.ds(pl.multiple_of(x * w, w), w)].astype(F32)
        total += lax.dot_general(full, panel, (((1,), (1,)), ((), ())),
                                 precision=lax.Precision.HIGHEST, preferred_element_type=F32)

    def share(buf, place, others):
        slot = links.take_recv(buf.shape[0])
        for device in others:
            links.copy(buf.at[place], buf.at[place], slot + place, *device)
        for d in range(1, buf.shape[0]):
            at = lax.rem(place + d, buf.shape[0])
            links.wait(buf.at[at], slot + at)
        out = buf[0]
        for k in range(1, buf.shape[0]):
            out += buf[k]
        return out

    ar = R.shape[1]
    C1[2 * x + i] = jnp.concatenate([total, jnp.zeros((ar, C1.shape[2] - ar), F32)], axis=1)
    total = share(C1, 2 * x + i, [(sib, x)] + [(2 * q + c, around[d]) for d in (1, 2, 3)
                                                for c in (0, 1)])
    if gy > 1:
        C2[qy] = total
        total = share(C2, qy, [(2 * g + i, x) for g in ys])
    if gz > 1:
        C3[qz] = total
        total = share(C3, qz, [(2 * g + i, x) for g in zs])
    corner[...] = cb[...] + total[:, :ar] / (4 * groups)
    links.drain()


def shards(precision_blocks, coupling, arrow_rows, corner_base):
    groups = lax.axis_size("tm") // 2
    levels = groups.bit_length() - 1
    n, w = precision_blocks.shape[1:]
    ar = arrow_rows.shape[1]
    h, hw = n // 2, w // 2
    vmem = pl.BlockSpec(memory_space=pltpu.VMEM)
    return pl.pallas_call(
        functools.partial(kernel, groups),
        out_shape=(
            jax.ShapeDtypeStruct(precision_blocks.shape, BF16),
            jax.ShapeDtypeStruct((2, ar, w), BF16),
            jax.ShapeDtypeStruct((ar, ar), F32),
        ),
        in_specs=[vmem] * 4,
        out_specs=(vmem,) * 3,
        scratch_shapes=[
            pltpu.VMEM((4, n, h), BF16),
            pltpu.VMEM((levels, n, h), BF16),
            pltpu.VMEM((levels + 5, 2, w, h), BF16),
            pltpu.VMEM((levels + 2, 2, w, h), BF16),
            pltpu.VMEM((levels + 7, X, 2, hw, w), BF16),
            pltpu.VMEM((levels + 7, 2, 2, hw, w), BF16),
            pltpu.VMEM((levels + 1, w, h), BF16),
            pltpu.VMEM((levels, 2, w, w), BF16),
            pltpu.VMEM((levels, 2, w, w), BF16),
            pltpu.VMEM((2, 2, w, w), BF16),
            pltpu.VMEM((4, w, h), BF16),
            pltpu.VMEM((2, hw, w), BF16),
            pltpu.VMEM((2, w, h), BF16),
            pltpu.VMEM((2, 2, w, w), BF16),
            pltpu.VMEM((2, h, w), BF16),
            pltpu.VMEM((8, ar, 128), F32),
            pltpu.VMEM((min(4, groups), ar, 128), F32),
            pltpu.VMEM((max(1, groups // 4), ar, 128), F32),
            pltpu.SemaphoreType.DMA((SENDS,)),
            pltpu.SemaphoreType.DMA((RECVS,)),
        ],
        compiler_params=pltpu.CompilerParams(
            collective_id=0, has_side_effects=True, vmem_limit_bytes=60 * 1024 * 1024),
        cost_estimate=pl.CostEstimate(
            flops=2 * 22 * w * n * n, bytes_accessed=4 << 20, transcendentals=0),
    )(precision_blocks, coupling, arrow_rows, corner_base)


def solution(mesh):
    return jax.shard_map(
        shards,
        mesh=mesh,
        in_specs=(P("tm", None, "col"), P("tm", "col", None), P("tm", None, None), P()),
        out_specs=(P("tm", None, "col"), P("tm", None, "col"), P()),
        check_vma=False,
    )
```

```python
import functools

import jax
import jax.numpy as jnp
from jax import lax
from jax.experimental import pallas as pl
from jax.experimental.pallas import tpu as pltpu
from jax.sharding import PartitionSpec as P

MESH = pl.DeviceIdType.MESH
BF16 = jnp.bfloat16
F32 = jnp.float32
X = 4
CHUNKS = 2
SEMS = 190


def dot(a, b):
    return jnp.dot(a, b, preferred_element_type=F32)


class Links:
    def __init__(self, sems):
        self.sems, self.used, self.pending = sems, 0, []

    def take(self, count=1):
        base = self.used
        self.used += count
        assert self.used <= SEMS
        return base

    def copy(self, src, dst, sent, got, tm, col, when=None):
        def start():
            pltpu.make_async_remote_copy(
                src_ref=src, dst_ref=dst, send_sem=self.sems.at[sent], recv_sem=self.sems.at[got],
                device_id=(tm, col), device_id_type=MESH).start()

        start() if when is None else pl.when(when)(start)

    def keep(self, src, dst, got, when=None):
        def start():
            pltpu.make_async_copy(src, dst, self.sems.at[got]).start()

        start() if when is None else pl.when(when)(start)

    def wait(self, ref, sem, when=None):
        def finish():
            pltpu.make_async_copy(ref, ref, self.sems.at[sem]).wait()

        finish() if when is None else pl.when(when)(finish)

    def later(self, ref, sem, when=None):
        self.pending.append((ref, sem, when))

    def drain(self):
        for ref, sem, when in self.pending:
            self.wait(ref, sem, when)


def kernel(groups, D, G, R, cb, sig, arrow, corner,
           GF, HA, HB, HC, HF, A, LA, LH, PS, PC, DC, DR, SB, RR, OT, C1, C2, C3, sems):
    n, w = D.shape[1], D.shape[2]
    h = n // 2
    m = w // 2
    hm = m // 2
    cm = m // CHUNKS
    levels = groups.bit_length() - 1
    gy = min(4, groups)
    gz = groups // gy
    tm, x = lax.axis_index("tm"), lax.axis_index("col")
    i = lax.rem(tm, 2)
    q = tm // 2
    sib = 2 * q + 1 - i
    me = 2 * x + i
    links = Links(sems)
    around = [lax.rem(x + d, X) for d in range(X)]
    right, left = around[1], around[3]
    ring = [(around[d], c) for d in (1, 3, 2) for c in (0, 1)]
    qy, qz = lax.rem(q, gy), q // gy
    ys = [(qz * gy + lax.rem(qy + d, gy)) for d in range(1, gy)]
    zs = [(lax.rem(qz + d, gz) * gy + qy) for d in range(1, gz)]

    def group_at(offset):
        return lax.rem(q + (offset + groups) % groups, groups)

    partners = [(sib, x)] + [(2 * q + c, chip) for chip, c in ring]
    offsets = set()
    for k in range(levels):
        offsets |= {(1 << k) % groups, (-(1 << k)) % groups}
    partners += [(2 * group_at(o) + i, x) for o in sorted(offsets)]
    partners += [(2 * g + i, x) for g in ys + zs]
    barrier = pltpu.get_barrier_semaphore()
    for partner in partners:
        pl.semaphore_signal(barrier, inc=1, device_id=partner, device_id_type=MESH)

    def rows(place, size=m, part=0):
        return pl.ds(pl.multiple_of(place * m + part * size, size), size)

    def panel(chip):
        return pl.ds(pl.multiple_of(chip * w, w), w)

    mine = rows(me)
    my_lanes = pl.ds(pl.multiple_of(i * m, m), m)
    its_lanes = pl.ds(pl.multiple_of((1 - i) * m, m), m)

    pair, its_pair = pl.ds(2 * i, 2), pl.ds(2 * (1 - i), 2)
    g_here, d_here, r_here = links.take(2), links.take(), links.take()
    for s in (0, 1):
        links.keep(G.at[s], GF.at[2 * i + s, panel(x)], g_here + s)
    for s in (0, 1):
        links.keep(D.at[s, :, my_lanes], DC.at[2 * i + s], d_here)
        links.keep(R.at[s], RR.at[2 * i + s], r_here)
    pl.semaphore_wait(barrier, len(partners))
    g_sent, g_near = links.take(), links.take(2)
    d_sent, d_near = links.take(), links.take()
    r_sent, r_near = links.take(), links.take()
    links.copy(G.at[0], GF.at[2 * i, panel(x)], g_sent, g_near, sib, x)
    links.copy(D.at[1, :, its_lanes], DC.at[2 * i + 1], d_sent, d_near, sib, x)
    links.copy(G.at[1], GF.at[2 * i + 1, panel(x)], g_sent, g_near + 1, sib, x)
    links.copy(D.at[0, :, its_lanes], DC.at[2 * i], d_sent, d_near, sib, x)
    for s in (0, 1):
        links.copy(R.at[s], RR.at[2 * i + s], r_sent, r_near, sib, x)
    links.later(GF.at[pair, panel(x)], g_sent)
    links.later(DC.at[pair], d_sent)
    links.later(RR.at[pair], r_sent)

    class Gather:
        def __init__(self, buf, own=True):
            self.buf, self.own = buf, own
            self.sent, self.got, self.near = links.take(), links.take(4), links.take()
            links.later(buf.at[pl.ds(0, (7 if own else 6) * m)], self.sent)

        def piece(self, chip, core, half):
            return self.buf.at[rows(2 * chip + core, hm, half)]

        def pass_on(self, ref, slot, chip):
            links.copy(ref, ref, self.sent, self.got + slot, tm, chip)

        def share(self, ref):
            links.copy(ref, ref, self.sent, self.near, sib, x)

        def start(self):
            top, bottom = self.piece(x, i, 0), self.piece(x, i, 1)
            self.pass_on(top, 0, right)
            self.pass_on(bottom, 1, left)
            self.pass_on(bottom, 2, right)
            self.pass_on(top, 2, left)
            if self.own:
                self.share(self.buf.at[mine])
            return self

        def mid(self):
            for ref, slot, chip in ((self.piece(left, i, 0), 0, right),
                                    (self.piece(right, i, 1), 1, left)):
                links.wait(ref, self.got + slot)
                self.pass_on(ref, 3, chip)
                self.share(ref)

        def end(self):
            opposite = around[2]
            for slot, refs in ((2, (self.piece(left, i, 1), self.piece(right, i, 0))),
                               (3, (self.piece(opposite, i, 0), self.piece(opposite, i, 1)))):
                links.wait(self.buf.at[mine], self.got + slot)
                for ref in refs:
                    self.share(ref)
            links.wait(self.buf.at[pl.ds(0, (4 if self.own else 3) * m)], self.near)

    class Turn:
        def __init__(self, stage, buf, parts):
            self.stage, self.buf, self.parts = stage, buf, parts
            self.sent, self.got = links.take(), links.take()
            links.later(stage.at[pl.ds(0, 2 * X - 1)], self.sent)

        def send(self, part, value):
            size = m // self.parts
            at = pl.ds(part * size, size)
            value = value.astype(BF16)
            for b in range(2 * X):
                self.stage[b, at] = value[:, b * m:(b + 1) * m]
            to = pl.ds(pl.multiple_of(me * m + part * size, size), size)
            for chip, c in ring:
                links.copy(self.stage.at[2 * chip + c, at], self.buf.at[to], self.sent, self.got,
                           2 * q + c, chip)
            links.copy(self.stage.at[2 * x + 1 - i, at], self.buf.at[to], self.sent, self.got,
                       sib, x)
            self.buf[to] = self.stage[me, at]

        def receive(self):
            links.wait(self.buf.at[pl.ds(0, (2 * X - 1) * m)], self.got)

        def turned(self):
            return self.buf[...].T

    turns = [0]

    def new_turn(parts=1):
        turns[0] += 1
        return Turn(PS.at[turns[0] - 1], PC.at[turns[0] - 1], parts)

    def turn_of(value):
        turn = new_turn()
        turn.send(0, value)
        return turn

    class Rows:
        def __init__(self, s, core, buf):
            self.s, self.sender, self.buf = s, i == core, buf
            self.sent, self.got = links.take(), links.take()

        def start(self):
            to = self.buf.at[:, panel(x)]
            for chip, c in ring + [(x, 1 - i)]:
                links.copy(D.at[self.s, rows(2 * chip + c)], to, self.sent, self.got,
                           2 * q + c, chip, self.sender)
            links.keep(D.at[self.s, mine], to, self.got, self.sender)
            links.later(D.at[self.s, pl.ds(0, (2 * X - 1) * m)], self.sent, self.sender)
            return self

        def receive(self):
            links.wait(self.buf, self.got)

    def column(t):
        return DC[t].T.astype(F32)

    def whole_product(out, L, H):
        sent, got = links.take(), links.take()
        for j in range(4):
            at = rows(4 * i + j)
            out[at] = dot(L[at], H[...]).astype(BF16)
            links.copy(out.at[at], out.at[at], sent, got, sib, x)
        links.later(out.at[pl.ds(pl.multiple_of(i * h, h), h)], sent)
        return lambda: links.wait(out.at[pl.ds(pl.multiple_of((1 - i) * h, h), h)], got)

    first0 = i == 0
    links.wait(GF.at[2 * i, panel(x)], g_here)
    links.wait(GF.at[2, panel(x)], g_near, first0)
    gather2 = Gather(GF.at[2], False).start()
    links.wait(GF.at[0, panel(x)], g_near, jnp.logical_not(first0))
    gather2.mid()
    gather0 = Gather(GF.at[0], False).start()
    rows2 = Rows(0, 1, DR.at[1]).start()
    links.wait(GF.at[2 * i + 1, panel(x)], g_here + 1)
    links.wait(GF.at[2 * (1 - i) + 1, panel(x)], g_near + 1)
    links.wait(DC.at[pair], d_here)
    links.wait(RR.at[pair], r_here)
    links.wait(DC.at[its_pair], d_near)
    links.wait(RR.at[its_pair], r_near)
    gather2.end()
    turn_b = turn_of(dot(DC[3].T, GF[2]))
    Hb = dot(GF[3, mine], GF[2]).astype(BF16)
    gather0.mid()
    gather1 = Gather(GF.at[1], False).start()
    gather0.end()
    rows2.receive()
    turn_b.receive()
    SB[0] = (DR[1].astype(F32) + dot(turn_b.turned(), GF[2])).astype(BF16)
    gather1.mid()
    rows1 = Rows(1, 0, DR.at[0]).start()
    gather1.end()
    got_ha = whole_product(HA, GF.at[1], GF.at[0])
    rows1.receive()
    turn_a = turn_of(dot(DR[0], GF[0]))
    got_ha()
    turn = turn_of(dot(SB[0], HA[...]))
    HF[0, mine] = dot(Hb, HA[...]).astype(BF16)
    gather = Gather(HF.at[0]).start()
    turn_a.receive()
    Sa = (column(0) + dot(turn_a.turned(), GF[0])).astype(BF16)

    def later_start(src, buf, e, keep, want, parts):
        sent, got, size = links.take(), links.take(parts), m // parts
        for c in range(parts):
            at = pl.ds(c * size, size)
            links.copy(src.at[at], buf.at[at], sent, got + c, 2 * group_at(-e) + i, x, keep)
        links.later(src, sent, keep)

        @pl.when(jnp.logical_not(want))
        def _():
            buf[...] = jnp.zeros_like(buf)

        return lambda c: links.wait(buf.at[pl.ds(c * size, size)], got + c, want)

    def send_state(src, buf, e):
        return later_start(src, buf, e, q >= e, q + e < groups, CHUNKS)

    def send_map(src, buf, e):
        return later_start(src, buf, e, jnp.logical_and(q >= e, q + e < groups),
                           q + 2 * e < groups, 1)

    def apply_later(got, L, H):
        turn = new_turn(CHUNKS)
        for c in range(CHUNKS):
            got(c)
            turn.send(c, dot(L[pl.ds(c * cm, cm)], H[...]))
        return turn

    got_h = send_map(HF.at[0, mine], LH.at[0], 1) if levels > 1 else None
    gather.mid()
    turn.receive()
    A[0] = (Sa.astype(F32) + dot(turn.turned(), HA[...])).astype(BF16)
    got_a = send_state(A.at[0], LA.at[0], 1)
    own = turn_of(A[0])
    for k in range(levels):
        final = k + 1 == levels
        e = 1 << k
        gather.end()
        if not final:
            got_h(0)
            HF[k + 1, mine] = dot(LH[k], HF[k]).astype(BF16)
            gather = Gather(HF.at[k + 1]).start()
            if k + 2 < levels:
                got_h = send_map(HF.at[k + 1, mine], LH.at[k + 1], 2 * e)
        else:
            gather = gather3 = Gather(GF.at[3], False).start()
            gather3.mid()
        turn = apply_later(got_a, LA.at[k], HF.at[k])
        if final:
            turn_c = turn_of(dot(SB[0], GF[1]))
            turn_s = turn_of(SB[0])
        else:
            gather.mid()
        own.receive()
        before = own.turned().astype(F32)
        turn.receive()
        A[k + 1] = (before + dot(turn.turned(), HF[k])).astype(BF16)
        got_a = send_state(A.at[k + 1], LA.at[k + 1], 1 if final else 2 * e)
        if not final:
            own = turn_of(A[k + 1])

    class RowsOut:
        def __init__(self, src, core, s):
            self.core, self.s, self.got = core, s, links.take()
            to, sent, near = sig.at[s, mine], links.take(), links.take()
            for d in (1, 3, 2):
                links.copy(src.at[:, panel(around[d])], to, sent, self.got, 2 * q + core, around[d])
            links.copy(src.at[:, panel(x)], to, near, self.got, sib, x, i != core)
            links.keep(src.at[:, panel(x)], to, self.got, i == core)
            links.later(src.at[:, pl.ds(0, 3 * w)], sent)
            links.later(src.at[:, panel(x)], near, i != core)

        def receive(self):
            links.wait(sig.at[self.s], self.got, i == self.core)

    class ColumnsOut:
        def __init__(self, stage, value, core, s):
            self.core, self.s, self.got, sent = core, s, links.take(), links.take()
            stage[...] = value.T
            links.copy(stage, sig.at[s, :, my_lanes], sent, self.got, sib, x, i != core)
            links.later(stage, sent, i != core)

            @pl.when(i == core)
            def _():
                sig[s, :, my_lanes] = stage[...]

        def receive(self):
            links.wait(sig.at[self.s, :, its_lanes], self.got, i == self.core)

    class Sum:
        def __init__(self, buf, place, value, others):
            size = buf.shape[0]
            self.buf, self.others, sent, self.got = (
                buf, buf.at[pl.ds(0, size - 1)], links.take(), links.take())
            buf[place] = value
            for device in others:
                links.copy(buf.at[place], buf.at[place], sent, self.got, *device)
            links.later(self.others, sent)

        def receive(self):
            links.wait(self.others, self.got)
            out = self.buf[0]
            for k in range(1, self.buf.shape[0]):
                out += self.buf[k]
            return out

    def small(a, b, dims):
        return lax.dot_general(a, b, (dims, ((), ())), precision=lax.Precision.HIGHEST,
                               preferred_element_type=F32)

    def by_lanes(a, b):
        return lax.dot_general(a, b, (((1,), (1,)), ((), ())), preferred_element_type=F32)

    out0 = RowsOut(A.at[levels], 0, 0)
    gather3.end()
    got_hb = whole_product(HB, GF.at[3], GF.at[2])
    got_hb()
    got_hc = whole_product(HC, HB, GF.at[1])
    turn_c.receive()
    SB[1] = (column(1) + dot(turn_c.turned(), GF[1])).astype(BF16)
    turn_s.receive()
    own_terms = {3: DC[3].T, 2: turn_s.turned(), 1: SB[1]}
    maps = {3: GF.at[3], 2: HB, 1: HC}
    ar = R.shape[1]
    my_arrow = [RR[t, :, pl.ds(pl.multiple_of(me * m, m), m)].astype(F32) for t in range(4)]
    total = small(my_arrow[0], by_lanes(A[levels], RR[0]), ((1,), (0,)))
    for t in (1, 2, 3):
        total += small(by_lanes(own_terms[t], RR[t]), my_arrow[t], ((0,), (1,)))
    got_hc()
    V = {t: by_lanes(RR[t], maps[t][mine]) for t in (1, 2, 3)}
    turns_out = {t: new_turn(CHUNKS) for t in (3, 2, 1)}
    products = []
    for c in range(CHUNKS):
        got_a(c)
        for t in (3, 2, 1):
            product = dot(LA[levels, pl.ds(c * cm, cm)], maps[t][...]).astype(BF16)
            turns_out[t].send(c, product)
            products.append((t, c, product))
    for t, c, product in products:
        total += small(V[t][:, c * cm:(c + 1) * cm], by_lanes(product, RR[t]), ((1,), (0,)))
    total = jnp.concatenate([total, jnp.zeros((ar, C1.shape[2] - ar), F32)], axis=1)
    total = Sum(C1, me, total, [(sib, x)] + [(2 * q + c, chip) for chip, c in ring]).receive()
    if gy > 1:
        total = Sum(C2, qy, total, [(2 * g + i, x) for g in ys]).receive()
    if gz > 1:
        corner_sum = Sum(C3, qz, total, [(2 * g + i, x) for g in zs])

    def sigma_of(t):
        turns_out[t].receive()
        value = (own_terms[t].astype(F32) + dot(turns_out[t].turned(), maps[t][...])).astype(BF16)
        return ColumnsOut(OT.at[t - 1], value, t // 2, t % 2)

    outs = [out0, sigma_of(3), sigma_of(2), sigma_of(1)]
    for out in outs:
        out.receive()
    for s in (0, 1):
        arrow[s] = dot(RR[2 * i + s], sig[s]).astype(BF16)
    if gz > 1:
        total = corner_sum.receive()
    corner[...] = cb[...] + total[:, :ar] / (4 * groups)
    links.drain()


def shards(precision_blocks, coupling, arrow_rows, corner_base):
    groups = lax.axis_size("tm") // 2
    levels = groups.bit_length() - 1
    assert levels % 2 == 1
    n, w = precision_blocks.shape[1:]
    ar = arrow_rows.shape[1]
    m = w // 2
    vmem = pl.BlockSpec(memory_space=pltpu.VMEM)
    far = pl.BlockSpec(memory_space=pl.ANY)
    turns = 2 * levels + 8
    return pl.pallas_call(
        functools.partial(kernel, groups),
        out_shape=(
            jax.ShapeDtypeStruct(precision_blocks.shape, BF16),
            jax.ShapeDtypeStruct((2, ar, w), BF16),
            jax.ShapeDtypeStruct((ar, ar), F32),
        ),
        in_specs=[far, far, far, vmem],
        out_specs=(vmem,) * 3,
        scratch_shapes=[
            pltpu.VMEM((4, n, n), BF16),
            pltpu.VMEM((n, n), BF16),
            pltpu.VMEM((n, n), BF16),
            pltpu.VMEM((n, n), BF16),
            pltpu.VMEM((levels, n, n), BF16),
            pltpu.VMEM((levels + 1, m, n), BF16),
            pltpu.VMEM((levels + 1, m, n), BF16),
            pltpu.VMEM((levels, m, n), BF16),
            pltpu.VMEM((turns, 2 * X, m, m), BF16),
            pltpu.VMEM((turns, n, m), BF16),
            pltpu.VMEM((4, n, m), BF16),
            pltpu.VMEM((2, m, n), BF16),
            pltpu.VMEM((2, m, n), BF16),
            pltpu.VMEM((4, ar, n), BF16),
            pltpu.VMEM((3, n, m), BF16),
            pltpu.VMEM((8, ar, 128), F32),
            pltpu.VMEM((min(4, groups), ar, 128), F32),
            pltpu.VMEM((max(1, groups // 4), ar, 128), F32),
            pltpu.SemaphoreType.DMA((SEMS,)),
        ],
        compiler_params=pltpu.CompilerParams(
            collective_id=0, has_side_effects=True, vmem_limit_bytes=60 * 1024 * 1024),
        cost_estimate=pl.CostEstimate(
            flops=2 * 22 * w * n * n, bytes_accessed=4 << 20, transcendentals=0),
    )(precision_blocks, coupling, arrow_rows, corner_base)


def solution(mesh):
    return jax.shard_map(
        shards,
        mesh=mesh,
        in_specs=(P("tm", None, "col"), P("tm", "col", None), P("tm", None, None), P()),
        out_specs=(P("tm", None, "col"), P("tm", None, "col"), P()),
        check_vma=False,
    )
```

```python
import functools

import jax
import jax.numpy as jnp
from jax import lax
from jax.experimental import pallas as pl
from jax.experimental.pallas import tpu as pltpu
from jax.sharding import PartitionSpec as P

MESH = pl.DeviceIdType.MESH
BF16 = jnp.bfloat16
F32 = jnp.float32
X = 4
PARTS = (1, 1, 1, 2, 2, 1)
SEMS = 159
FIRST = (0, 1, 2)


def dot(a, b):
    return jnp.dot(a, b, preferred_element_type=F32)


class Links:
    def __init__(self, sems):
        self.sems, self.used, self.pending = sems, 0, []

    def take(self, count=1):
        base = self.used
        self.used += count
        assert self.used <= SEMS
        return base

    def copy(self, src, dst, sent, got, tm, col, when=None):
        def start():
            pltpu.make_async_remote_copy(
                src_ref=src, dst_ref=dst, send_sem=self.sems.at[sent], recv_sem=self.sems.at[got],
                device_id=(tm, col), device_id_type=MESH).start()

        start() if when is None else pl.when(when)(start)

    def keep(self, src, dst, got, when=None):
        def start():
            pltpu.make_async_copy(src, dst, self.sems.at[got]).start()

        start() if when is None else pl.when(when)(start)

    def wait(self, ref, sem, when=None):
        def finish():
            pltpu.make_async_copy(ref, ref, self.sems.at[sem]).wait()

        finish() if when is None else pl.when(when)(finish)

    def later(self, ref, sem, when=None):
        self.pending.append((ref, sem, when))

    def drain(self):
        for ref, sem, when in self.pending:
            self.wait(ref, sem, when)


def kernel(groups, D, G, R, cb, sig, arrow, corner,
           GF, HA, HB, HC, H0, HF, A, LA, LH, PS, PC, DC, DR, SB, RR, OT, C1, C2, C3, sems):
    n, w = D.shape[1], D.shape[2]
    h = n // 2
    m = w // 2
    hm = m // 2
    levels = groups.bit_length() - 1
    gy = min(4, groups)
    gz = groups // gy
    tm, x = lax.axis_index("tm"), lax.axis_index("col")
    i = lax.rem(tm, 2)
    q = tm // 2
    sib = 2 * q + 1 - i
    me = 2 * x + i
    links = Links(sems)
    around = [lax.rem(x + d, X) for d in range(X)]
    right, left = around[1], around[3]
    ring = [(around[d], c) for d in (1, 3, 2) for c in (0, 1)]
    qy, qz = lax.rem(q, gy), q // gy
    ys = [(qz * gy + lax.rem(qy + d, gy)) for d in range(1, gy)]
    zs = [(lax.rem(qz + d, gz) * gy + qy) for d in range(1, gz)]

    def group_at(offset):
        return lax.rem(q + (offset + groups) % groups, groups)

    partners = [(sib, x)] + [(2 * q + c, chip) for chip, c in ring]
    offsets = set()
    for k in range(levels):
        offsets |= {(1 << k) % groups, (-(1 << k)) % groups}
    partners += [(2 * group_at(o) + i, x) for o in sorted(offsets)]
    partners += [(2 * g + i, x) for g in ys + zs]
    barrier = pltpu.get_barrier_semaphore()
    for partner in partners:
        pl.semaphore_signal(barrier, inc=1, device_id=partner, device_id_type=MESH)

    def rows(place, size=m, part=0):
        return pl.ds(pl.multiple_of(place * m + part * size, size), size)

    def panel(chip):
        return pl.ds(pl.multiple_of(chip * w, w), w)

    mine = rows(me)
    my_rows = pl.ds(pl.multiple_of(i * h, h), h)
    its_rows = pl.ds(pl.multiple_of((1 - i) * h, h), h)
    my_lanes = pl.ds(pl.multiple_of(i * m, m), m)
    its_lanes = pl.ds(pl.multiple_of((1 - i) * m, m), m)

    pair, its_pair = pl.ds(2 * i, 2), pl.ds(2 * (1 - i), 2)
    g_here, d_here, r_here = links.take(2), links.take(), links.take()
    for s in (0, 1):
        links.keep(G.at[s], GF.at[2 * i + s, panel(x)], g_here + s)
    for s in (0, 1):
        links.keep(D.at[s, :, my_lanes], DC.at[2 * i + s], d_here)
        links.keep(R.at[s], RR.at[2 * i + s], r_here)
    pl.semaphore_wait(barrier, len(partners))
    g_sent, g_near = links.take(), links.take(2)
    d_sent, d_near = links.take(), links.take()
    r_sent, r_near = links.take(), links.take()
    links.copy(G.at[0], GF.at[2 * i, panel(x)], g_sent, g_near, sib, x)
    links.copy(D.at[1, :, its_lanes], DC.at[2 * i + 1], d_sent, d_near, sib, x)
    links.copy(G.at[1], GF.at[2 * i + 1, panel(x)], g_sent, g_near + 1, sib, x)
    links.copy(D.at[0, :, its_lanes], DC.at[2 * i], d_sent, d_near, sib, x)
    for s in (0, 1):
        links.copy(R.at[s], RR.at[2 * i + s], r_sent, r_near, sib, x)
    links.later(GF.at[pair, panel(x)], g_sent)
    links.later(DC.at[pair], d_sent)
    links.later(RR.at[pair], r_sent)

    class Gather:
        def __init__(self, buf, own=True):
            self.buf, self.own = buf, own
            self.sent, self.got, self.near = links.take(), links.take(4), links.take()
            links.later(buf.at[pl.ds(0, (7 if own else 6) * m)], self.sent)

        def piece(self, chip, core, half):
            return self.buf.at[rows(2 * chip + core, hm, half)]

        def pass_on(self, ref, slot, chip):
            links.copy(ref, ref, self.sent, self.got + slot, tm, chip)

        def share(self, ref):
            links.copy(ref, ref, self.sent, self.near, sib, x)

        def start(self):
            top, bottom = self.piece(x, i, 0), self.piece(x, i, 1)
            self.pass_on(top, 0, right)
            self.pass_on(bottom, 1, left)
            self.pass_on(bottom, 2, right)
            self.pass_on(top, 2, left)
            if self.own:
                self.share(self.buf.at[mine])
            return self

        def mid(self):
            for ref, slot, chip in ((self.piece(left, i, 0), 0, right),
                                    (self.piece(right, i, 1), 1, left)):
                links.wait(ref, self.got + slot)
                self.pass_on(ref, 3, chip)
                self.share(ref)

        def end(self):
            opposite = around[2]
            for slot, refs in ((2, (self.piece(left, i, 1), self.piece(right, i, 0))),
                               (3, (self.piece(opposite, i, 0), self.piece(opposite, i, 1)))):
                links.wait(self.buf.at[mine], self.got + slot)
                for ref in refs:
                    self.share(ref)
            links.wait(self.buf.at[pl.ds(0, (4 if self.own else 3) * m)], self.near)

    t_sent = links.take()

    class Turn:
        def __init__(self, stage, buf, parts):
            self.stage, self.buf, self.parts = stage, buf, parts
            self.sent, self.got = t_sent, links.take()

        def send(self, part, value, half=None):
            size = m // self.parts
            at = pl.ds(part * size, size)
            value = value.astype(BF16)
            to = pl.ds(pl.multiple_of(me * m + part * size, size), size)
            if half is None:
                for b in range(2 * X):
                    self.stage[b, at] = value[:, b * m:(b + 1) * m]
                for chip, c in ring + [(x, 1 - i)]:
                    links.copy(self.stage.at[2 * chip + c, at], self.buf.at[to], self.sent,
                               self.got, 2 * q + c, chip)
                self.buf[to] = self.stage[me, at]
                return
            for b in range(X):
                self.stage[X * half + b, at] = value[:, b * m:(b + 1) * m]
            for b in range(X * half, X * half + X):
                links.copy(self.stage.at[b, at], self.buf.at[to], self.sent, self.got,
                           2 * q + b % 2, b // 2, b != me)

            @pl.when(me // X == half)
            def _():
                self.buf[to] = self.stage[me, at]

        def receive(self):
            links.wait(self.buf.at[pl.ds(0, (2 * X - 1) * m)], self.got)

        def turned(self):
            return self.buf[...].T

    turns = [0]

    def new_turn(parts=1):
        turns[0] += 1
        return Turn(PS.at[turns[0] - 1], PC.at[turns[0] - 1], parts)

    def turn_of(value):
        turn = new_turn()
        turn.send(0, value)
        return turn

    class Rows:
        def __init__(self, s, core, buf):
            self.s, self.sender, self.buf = s, i == core, buf
            self.sent, self.got = links.take(), links.take()

        def start(self):
            to = self.buf.at[:, panel(x)]
            for chip, c in ring + [(x, 1 - i)]:
                links.copy(D.at[self.s, rows(2 * chip + c)], to, self.sent, self.got,
                           2 * q + c, chip, self.sender)
            links.keep(D.at[self.s, mine], to, self.got, self.sender)
            links.later(D.at[self.s, pl.ds(0, (2 * X - 1) * m)], self.sent, self.sender)
            return self

        def receive(self):
            links.wait(self.buf, self.got)

    def column(t):
        return DC[t].T.astype(F32)

    def whole_product(out, L, H):
        sent, got = links.take(), links.take()
        for j in range(4):
            at = rows(4 * i + j)
            out[at] = dot(L[at], H[...]).astype(BF16)
            links.copy(out.at[at], out.at[at], sent, got, sib, x)
        links.later(out.at[my_rows], sent)
        return lambda: links.wait(out.at[its_rows], got)

    first0 = i == 0
    links.wait(GF.at[2 * i, panel(x)], g_here)
    links.wait(GF.at[2, panel(x)], g_near, first0)
    gather2 = Gather(GF.at[2], False).start()
    links.wait(GF.at[0, panel(x)], g_near, jnp.logical_not(first0))
    gather2.mid()
    gather0 = Gather(GF.at[0], False).start()
    rows2 = Rows(0, 1, DR.at[1]).start()
    links.wait(GF.at[2 * i + 1, panel(x)], g_here + 1)
    links.wait(GF.at[2 * (1 - i) + 1, panel(x)], g_near + 1)
    links.wait(DC.at[pair], d_here)
    links.wait(RR.at[pair], r_here)
    links.wait(DC.at[its_pair], d_near)
    links.wait(RR.at[its_pair], r_near)
    gather2.end()
    turn_b = turn_of(dot(DC[3].T, GF[2]))
    Hb = dot(GF[3, mine], GF[2]).astype(BF16)
    gather0.mid()
    gather1 = Gather(GF.at[1], False).start()
    gather0.end()
    rows2.receive()
    turn_b.receive()
    SB[0] = (DR[1].astype(F32) + dot(turn_b.turned(), GF[2])).astype(BF16)
    gather1.mid()
    rows1 = Rows(1, 0, DR.at[0]).start()
    def later_start(src, buf, e, keep, want, parts):
        sent, got, size = links.take(), links.take(parts), m // parts
        for c in range(parts):
            at = pl.ds(c * size, size)
            links.copy(src.at[at], buf.at[at], sent, got + c, 2 * group_at(-e) + i, x, keep)
        links.later(src, sent, keep)

        @pl.when(jnp.logical_not(want))
        def _():
            buf[...] = jnp.zeros_like(buf)

        return lambda c: links.wait(buf.at[pl.ds(c * size, size)], got + c, want)

    def send_state(k):
        e = 1 if k == levels else 1 << k
        return later_start(A.at[k], LA.at[k], e, q >= e, q + e < groups, PARTS[k])

    def send_map(k, half):
        e = 1 << k
        return later_start(HF.at[k, half, mine] if k else H0.at[half], LH.at[k, :, pl.ds(half * h, h)], e,
                           jnp.logical_and(q >= e, q + e < groups), q + 2 * e < groups, 1)

    gather1.end()
    gather3 = Gather(GF.at[3], False).start()
    rows1.receive()
    turn_a = turn_of(dot(DR[0], GF[0]))
    whole_product(HA, GF.at[1], GF.at[0])()
    turn = turn_of(dot(SB[0], HA[...]))
    for half in (0, 1):
        H0[half] = dot(Hb, HA[:, half * h:half * h + h]).astype(BF16)
    got_h = [send_map(0, half) for half in (0, 1)] if levels > 1 else []
    turn_a.receive()
    Sa = (column(0) + dot(turn_a.turned(), GF[0])).astype(BF16)
    gather3.mid()
    turn.receive()
    A[0] = (Sa.astype(F32) + dot(turn.turned(), HA[...])).astype(BF16)
    got_a = send_state(0)
    own = turn_of(A[0])
    turn_c = turn_of(dot(SB[0], GF[1]))
    turn_s = turn_of(SB[0])
    gather3.end()
    got_hb = whole_product(HB, GF.at[3], GF.at[2])
    sent, got = links.take(), links.take()
    for j in range(4):
        at = rows(4 * i + j)
        for half in (0, 1):
            HF[0, half, at] = dot(HB[at], HA[:, half * h:half * h + h]).astype(BF16)
        links.copy(HF.at[0, :, at], HF.at[0, :, at], sent, got, sib, x)
    links.later(HF.at[0, :, my_rows], sent)
    links.wait(HF.at[0, :, its_rows], got)
    gathers = []
    def small(a, b, dims):
        return lax.dot_general(a, b, (dims, ((), ())), precision=lax.Precision.HIGHEST,
                               preferred_element_type=F32)

    def by_lanes(a, b):
        return lax.dot_general(a, b, (((1,), (1,)), ((), ())), preferred_element_type=F32)

    ar = R.shape[1]
    maps = {3: GF.at[3], 2: HB, 1: HC}
    ready = {}

    def prepare(k):
        if k == max(levels - 2, 0):
            got_hb()
            ready["hc"] = whole_product(HC, HB, GF.at[1])
        if k == levels - 1:
            ready["hc"]()
            turn_c.receive()
            SB[1] = (column(1) + dot(turn_c.turned(), GF[1])).astype(BF16)
            turn_s.receive()
            ready["own"] = {3: DC[3].T, 2: turn_s.turned(), 1: SB[1]}
            lanes = [RR[t, :, pl.ds(pl.multiple_of(me * m, m), m)].astype(F32)
                     for t in range(4)]
            ready["lanes"] = lanes[0]
            ready["total"] = sum(
                small(by_lanes(ready["own"][t], RR[t]), lanes[t], ((0,), (1,)))
                for t in (1, 2, 3))
            ready["V"] = {t: by_lanes(RR[t], maps[t][mine]) for t in (1, 2, 3)}

    for k in range(levels):
        final = k + 1 == levels
        ends, gathers, got = gathers, [], []
        def compose(half):
            HF[k + 1, half, mine] = dot(LH[k], HF[k, half]).astype(BF16)
            gathers.append(Gather(HF.at[k + 1, half]).start())
            if k + 2 < levels:
                got.append(send_map(k + 1, half))

        def apply():
            size = m // PARTS[k]
            for c in range(PARTS[k]):
                got_a(c)
                for half in (0, 1):
                    turn.send(c, dot(LA[k, pl.ds(c * size, size)], HF[k, half]), half)

        turn = new_turn(PARTS[k])
        if k == 0:
            apply()
            if not final:
                for received in got_h:
                    received(0)
                compose(0)
                compose(1)
        else:
            ends[0].end()
            if not final:
                for received in got_h:
                    received(0)
                compose(0)
            ends[1].end()
            if k not in FIRST and not final:
                compose(1)
            if k + 1 >= levels - 1:
                prepare(k)
            apply()
            if k in FIRST and not final:
                compose(1)
        got_h = got
        if not final:
            gathers[0].mid()
        if k + 2 == levels:
            gathers[1].mid()
        own.receive()
        before = own.turned().astype(F32)
        turn.receive()
        columns = turn.turned()
        for half in (0, 1):
            at = pl.ds(half * h, h)
            A[k + 1, :, at] = (before[:, half * h:half * h + h]
                               + dot(columns, HF[k, half])).astype(BF16)
        got_a = send_state(k + 1)
        if not final:
            own = turn_of(A[k + 1])
            if k + 2 != levels:
                gathers[1].mid()

    class RowsOut:
        def __init__(self, src, core, s):
            self.core, self.s, self.got = core, s, links.take()
            to, sent, near = sig.at[s, mine], links.take(), links.take()
            for d in (1, 3, 2):
                links.copy(src.at[:, panel(around[d])], to, sent, self.got, 2 * q + core, around[d])
            links.copy(src.at[:, panel(x)], to, near, self.got, sib, x, i != core)
            links.keep(src.at[:, panel(x)], to, self.got, i == core)
            links.later(src.at[:, pl.ds(0, 3 * w)], sent)
            links.later(src.at[:, panel(x)], near, i != core)

        def receive(self):
            links.wait(sig.at[self.s], self.got, i == self.core)

    class ColumnsOut:
        def __init__(self, stage, value, core, s):
            self.core, self.s, self.got, sent = core, s, links.take(), links.take()
            stage[...] = value.T
            links.copy(stage, sig.at[s, :, my_lanes], sent, self.got, sib, x, i != core)
            links.later(stage, sent, i != core)

            @pl.when(i == core)
            def _():
                sig[s, :, my_lanes] = stage[...]

        def receive(self):
            links.wait(sig.at[self.s, :, its_lanes], self.got, i == self.core)

    class Sum:
        def __init__(self, buf, place, value, others):
            size = buf.shape[0]
            self.buf, self.others, sent, self.got = (
                buf, buf.at[pl.ds(0, size - 1)], links.take(), links.take())
            buf[place] = value
            for device in others:
                links.copy(buf.at[place], buf.at[place], sent, self.got, *device)
            links.later(self.others, sent)

        def receive(self):
            links.wait(self.others, self.got)
            out = self.buf[0]
            for k in range(1, self.buf.shape[0]):
                out += self.buf[k]
            return out

    if levels == 1:
        prepare(0)
    out0 = RowsOut(A.at[levels], 0, 0)
    own_terms, V = ready["own"], ready["V"]
    total = ready["total"] + small(ready["lanes"], by_lanes(A[levels], RR[0]), ((1,), (0,)))
    turns_out = {t: new_turn(PARTS[levels]) for t in (3, 2, 1)}
    assert PARTS[levels] == 1
    got_a(0)
    products = {}
    for t in (3, 2, 1):
        products[t] = dot(LA[levels], maps[t][...]).astype(BF16)
        if t == 3:
            turns_out[t].send(0, products[t])
    for t in (1, 2, 3):
        total += small(V[t], by_lanes(products[t], RR[t]), ((1,), (0,)))
    total = jnp.concatenate([total, jnp.zeros((ar, C1.shape[2] - ar), F32)], axis=1)
    corner_sum = Sum(C1, me, total, [(sib, x)] + [(2 * q + c, chip) for chip, c in ring])
    for t in (2, 1):
        turns_out[t].send(0, products[t])

    def sigma_of(t):
        turns_out[t].receive()
        value = (own_terms[t].astype(F32) + dot(turns_out[t].turned(), maps[t][...])).astype(BF16)
        return ColumnsOut(OT.at[t - 1], value, t // 2, t % 2)

    outs = [out0]
    total = corner_sum.receive()
    if gy > 1:
        corner_sum = Sum(C2, qy, total, [(2 * g + i, x) for g in ys])
    outs += [sigma_of(3), sigma_of(2)]
    if gy > 1:
        total = corner_sum.receive()
    if gz > 1:
        corner_sum = Sum(C3, qz, total, [(2 * g + i, x) for g in zs])
    outs.append(sigma_of(1))
    for out in outs:
        out.receive()
    for s in (0, 1):
        arrow[s] = dot(RR[2 * i + s], sig[s]).astype(BF16)
    if gz > 1:
        total = corner_sum.receive()
    corner[...] = cb[...] + total[:, :ar] / (4 * groups)
    links.later(PS.at[pl.ds(0, turns[0]), pl.ds(0, 2 * X - 1)], t_sent)
    links.drain()


def passed_on(*refs):
    count = len(refs) // 2
    for src, dst in zip(refs[:count], refs[count:]):
        dst[...] = src[...]


def shards(precision_blocks, coupling, arrow_rows, corner_base):
    groups = lax.axis_size("tm") // 2
    levels = groups.bit_length() - 1
    assert levels % 2 == 1
    n, w = precision_blocks.shape[1:]
    ar = arrow_rows.shape[1]
    h, m = n // 2, w // 2
    vmem = pl.BlockSpec(memory_space=pltpu.VMEM)
    far = pl.BlockSpec(memory_space=pl.ANY)
    turns = 2 * levels + 8
    shapes = (
        jax.ShapeDtypeStruct(precision_blocks.shape, BF16),
        jax.ShapeDtypeStruct((2, ar, w), BF16),
        jax.ShapeDtypeStruct((ar, ar), F32),
    )
    results = pl.pallas_call(
        functools.partial(kernel, groups),
        out_shape=shapes,
        in_specs=[far, far, far, vmem],
        out_specs=(vmem,) * 3,
        scratch_shapes=[
            pltpu.VMEM((4, n, n), BF16),
            pltpu.VMEM((n, n), BF16),
            pltpu.VMEM((n, n), BF16),
            pltpu.VMEM((n, n), BF16),
            pltpu.VMEM((2, m, n // 2), BF16),
            pltpu.VMEM((levels, 2, n, h), BF16),
            pltpu.VMEM((levels + 1, m, n), BF16),
            pltpu.VMEM((levels + 1, m, n), BF16),
            pltpu.VMEM((levels, m, n), BF16),
            pltpu.VMEM((turns, 2 * X, m, m), BF16),
            pltpu.VMEM((turns, n, m), BF16),
            pltpu.VMEM((4, n, m), BF16),
            pltpu.VMEM((2, m, n), BF16),
            pltpu.VMEM((2, m, n), BF16),
            pltpu.VMEM((4, ar, n), BF16),
            pltpu.VMEM((3, n, m), BF16),
            pltpu.VMEM((8, ar, 128), F32),
            pltpu.VMEM((min(4, groups), ar, 128), F32),
            pltpu.VMEM((max(1, groups // 4), ar, 128), F32),
            pltpu.SemaphoreType.DMA((SEMS,)),
        ],
        compiler_params=pltpu.CompilerParams(
            collective_id=0, has_side_effects=True, vmem_limit_bytes=60 * 1024 * 1024),
        cost_estimate=pl.CostEstimate(
            flops=2 * 22 * w * n * n, bytes_accessed=4 << 20, transcendentals=0),
    )(precision_blocks, coupling, arrow_rows, corner_base)
    return pl.pallas_call(
        passed_on,
        out_shape=shapes,
        in_specs=[vmem] * 3,
        out_specs=(vmem,) * 3,
    )(*results)


def solution(mesh):
    return jax.shard_map(
        shards,
        mesh=mesh,
        in_specs=(P("tm", None, "col"), P("tm", "col", None), P("tm", None, None), P()),
        out_specs=(P("tm", None, "col"), P("tm", None, "col"), P()),
        check_vma=False,
    )
```

```python
import functools

import jax
import jax.numpy as jnp
from jax import lax
from jax.experimental import pallas as pl
from jax.experimental.pallas import tpu as pltpu
from jax.sharding import PartitionSpec as P

MESH = pl.DeviceIdType.MESH
BF16 = jnp.bfloat16
F32 = jnp.float32
X = 4
PARTS = (1, 1, 1, 2, 2, 2)
SEMS = 160
FIRST = (0, 1, 2)


def dot(a, b):
    return jnp.dot(a, b, preferred_element_type=F32)


class Links:
    def __init__(self, sems):
        self.sems, self.used, self.pending = sems, 0, []

    def take(self, count=1):
        base = self.used
        self.used += count
        assert self.used <= SEMS
        return base

    def copy(self, src, dst, sent, got, tm, col, when=None):
        def start():
            pltpu.make_async_remote_copy(
                src_ref=src, dst_ref=dst, send_sem=self.sems.at[sent], recv_sem=self.sems.at[got],
                device_id=(tm, col), device_id_type=MESH).start()

        start() if when is None else pl.when(when)(start)

    def keep(self, src, dst, got, when=None):
        def start():
            pltpu.make_async_copy(src, dst, self.sems.at[got]).start()

        start() if when is None else pl.when(when)(start)

    def wait(self, ref, sem, when=None):
        def finish():
            pltpu.make_async_copy(ref, ref, self.sems.at[sem]).wait()

        finish() if when is None else pl.when(when)(finish)

    def later(self, ref, sem, when=None):
        self.pending.append((ref, sem, when))

    def drain(self):
        for ref, sem, when in self.pending:
            self.wait(ref, sem, when)


def kernel(groups, D, G, R, cb, sig, arrow, corner,
           GF, HA, HB, HC, H0, HF, A, LA, LH, PS, PC, DC, DR, SB, RR, OT, C1, C2, C3, sems):
    n, w = D.shape[1], D.shape[2]
    h = n // 2
    m = w // 2
    hm = m // 2
    levels = groups.bit_length() - 1
    gy = min(4, groups)
    gz = groups // gy
    tm, x = lax.axis_index("tm"), lax.axis_index("col")
    i = lax.rem(tm, 2)
    q = tm // 2
    sib = 2 * q + 1 - i
    me = 2 * x + i
    links = Links(sems)
    around = [lax.rem(x + d, X) for d in range(X)]
    right, left = around[1], around[3]
    ring = [(around[d], c) for d in (1, 3, 2) for c in (0, 1)]
    qy, qz = lax.rem(q, gy), q // gy
    ys = [(qz * gy + lax.rem(qy + d, gy)) for d in range(1, gy)]
    zs = [(lax.rem(qz + d, gz) * gy + qy) for d in range(1, gz)]

    def group_at(offset):
        return lax.rem(q + (offset + groups) % groups, groups)

    partners = [(sib, x)] + [(2 * q + c, chip) for chip, c in ring]
    offsets = set()
    for k in range(levels):
        offsets |= {(1 << k) % groups, (-(1 << k)) % groups}
    partners += [(2 * group_at(o) + i, x) for o in sorted(offsets)]
    partners += [(2 * g + i, x) for g in ys + zs]
    barrier = pltpu.get_barrier_semaphore()
    for partner in partners:
        pl.semaphore_signal(barrier, inc=1, device_id=partner, device_id_type=MESH)

    def rows(place, size=m, part=0):
        return pl.ds(pl.multiple_of(place * m + part * size, size), size)

    def panel(chip):
        return pl.ds(pl.multiple_of(chip * w, w), w)

    mine = rows(me)
    my_rows = pl.ds(pl.multiple_of(i * h, h), h)
    its_rows = pl.ds(pl.multiple_of((1 - i) * h, h), h)
    my_lanes = pl.ds(pl.multiple_of(i * m, m), m)
    its_lanes = pl.ds(pl.multiple_of((1 - i) * m, m), m)

    pair, its_pair = pl.ds(2 * i, 2), pl.ds(2 * (1 - i), 2)
    g_here, d_here, r_here = links.take(2), links.take(), links.take()
    for s in (0, 1):
        links.keep(G.at[s], GF.at[2 * i + s, panel(x)], g_here + s)
    for s in (0, 1):
        links.keep(D.at[s, :, my_lanes], DC.at[2 * i + s], d_here)
        links.keep(R.at[s], RR.at[2 * i + s], r_here)
    pl.semaphore_wait(barrier, len(partners))
    g_sent, g_near = links.take(), links.take(2)
    d_sent, d_near = links.take(), links.take()
    r_sent, r_near = links.take(), links.take()
    links.copy(G.at[0], GF.at[2 * i, panel(x)], g_sent, g_near, sib, x)
    links.copy(D.at[1, :, its_lanes], DC.at[2 * i + 1], d_sent, d_near, sib, x)
    links.copy(G.at[1], GF.at[2 * i + 1, panel(x)], g_sent, g_near + 1, sib, x)
    links.copy(D.at[0, :, its_lanes], DC.at[2 * i], d_sent, d_near, sib, x)
    for s in (0, 1):
        links.copy(R.at[s], RR.at[2 * i + s], r_sent, r_near, sib, x)
    links.later(GF.at[pair, panel(x)], g_sent)
    links.later(DC.at[pair], d_sent)
    links.later(RR.at[pair], r_sent)

    class Gather:
        def __init__(self, buf, own=True):
            self.buf, self.own = buf, own
            self.sent, self.got, self.near = links.take(), links.take(4), links.take()
            links.later(buf.at[pl.ds(0, (7 if own else 6) * m)], self.sent)

        def piece(self, chip, core, half):
            return self.buf.at[rows(2 * chip + core, hm, half)]

        def pass_on(self, ref, slot, chip):
            links.copy(ref, ref, self.sent, self.got + slot, tm, chip)

        def share(self, ref):
            links.copy(ref, ref, self.sent, self.near, sib, x)

        def start(self):
            top, bottom = self.piece(x, i, 0), self.piece(x, i, 1)
            self.pass_on(top, 0, right)
            self.pass_on(bottom, 1, left)
            self.pass_on(bottom, 2, right)
            self.pass_on(top, 2, left)
            if self.own:
                self.share(self.buf.at[mine])
            return self

        def mid(self):
            for ref, slot, chip in ((self.piece(left, i, 0), 0, right),
                                    (self.piece(right, i, 1), 1, left)):
                links.wait(ref, self.got + slot)
                self.pass_on(ref, 3, chip)
                self.share(ref)

        def end(self):
            opposite = around[2]
            for slot, refs in ((2, (self.piece(left, i, 1), self.piece(right, i, 0))),
                               (3, (self.piece(opposite, i, 0), self.piece(opposite, i, 1)))):
                links.wait(self.buf.at[mine], self.got + slot)
                for ref in refs:
                    self.share(ref)
            links.wait(self.buf.at[pl.ds(0, (4 if self.own else 3) * m)], self.near)

    t_sent = links.take()

    class Turn:
        def __init__(self, stage, buf, parts):
            self.stage, self.buf, self.parts = stage, buf, parts
            self.sent, self.got = t_sent, links.take()

        def send(self, part, value, half=None):
            size = m // self.parts
            at = pl.ds(part * size, size)
            value = value.astype(BF16)
            to = pl.ds(pl.multiple_of(me * m + part * size, size), size)
            if half is None:
                for b in range(2 * X):
                    self.stage[b, at] = value[:, b * m:(b + 1) * m]
                for chip, c in ring + [(x, 1 - i)]:
                    links.copy(self.stage.at[2 * chip + c, at], self.buf.at[to], self.sent,
                               self.got, 2 * q + c, chip)
                self.buf[to] = self.stage[me, at]
                return
            for b in range(X):
                self.stage[X * half + b, at] = value[:, b * m:(b + 1) * m]
            for b in range(X * half, X * half + X):
                links.copy(self.stage.at[b, at], self.buf.at[to], self.sent, self.got,
                           2 * q + b % 2, b // 2, b != me)

            @pl.when(me // X == half)
            def _():
                self.buf[to] = self.stage[me, at]

        def receive(self):
            links.wait(self.buf.at[pl.ds(0, (2 * X - 1) * m)], self.got)

        def turned(self):
            return self.buf[...].T

    turns = [0]

    def new_turn(parts=1):
        turns[0] += 1
        return Turn(PS.at[turns[0] - 1], PC.at[turns[0] - 1], parts)

    def turn_of(value):
        turn = new_turn()
        turn.send(0, value)
        return turn

    class Rows:
        def __init__(self, s, core, buf):
            self.s, self.sender, self.buf = s, i == core, buf
            self.sent, self.got = links.take(), links.take()

        def start(self):
            to = self.buf.at[:, panel(x)]
            for chip, c in ring + [(x, 1 - i)]:
                links.copy(D.at[self.s, rows(2 * chip + c)], to, self.sent, self.got,
                           2 * q + c, chip, self.sender)
            links.keep(D.at[self.s, mine], to, self.got, self.sender)
            links.later(D.at[self.s, pl.ds(0, (2 * X - 1) * m)], self.sent, self.sender)
            return self

        def receive(self):
            links.wait(self.buf, self.got)

    def column(t):
        return DC[t].T.astype(F32)

    def whole_product(out, L, H):
        sent, got = links.take(), links.take()
        for j in range(4):
            at = rows(4 * i + j)
            out[at] = dot(L[at], H[...]).astype(BF16)
            links.copy(out.at[at], out.at[at], sent, got, sib, x)
        links.later(out.at[my_rows], sent)
        return lambda: links.wait(out.at[its_rows], got)

    first0 = i == 0
    links.wait(GF.at[2 * i, panel(x)], g_here)
    links.wait(GF.at[2, panel(x)], g_near, first0)
    gather2 = Gather(GF.at[2], False).start()
    links.wait(GF.at[0, panel(x)], g_near, jnp.logical_not(first0))
    gather2.mid()
    gather0 = Gather(GF.at[0], False).start()
    rows2 = Rows(0, 1, DR.at[1]).start()
    links.wait(GF.at[2 * i + 1, panel(x)], g_here + 1)
    links.wait(GF.at[2 * (1 - i) + 1, panel(x)], g_near + 1)
    links.wait(DC.at[pair], d_here)
    links.wait(RR.at[pair], r_here)
    links.wait(DC.at[its_pair], d_near)
    links.wait(RR.at[its_pair], r_near)
    gather2.end()
    turn_b = turn_of(dot(DC[3].T, GF[2]))
    Hb = dot(GF[3, mine], GF[2]).astype(BF16)
    gather0.mid()
    gather1 = Gather(GF.at[1], False).start()
    gather0.end()
    rows2.receive()
    turn_b.receive()
    SB[0] = (DR[1].astype(F32) + dot(turn_b.turned(), GF[2])).astype(BF16)
    gather1.mid()
    rows1 = Rows(1, 0, DR.at[0]).start()
    def later_start(src, buf, e, keep, want, parts):
        sent, got, size = links.take(), links.take(parts), m // parts
        for c in range(parts):
            at = pl.ds(c * size, size)
            links.copy(src.at[at], buf.at[at], sent, got + c, 2 * group_at(-e) + i, x, keep)
        links.later(src, sent, keep)

        @pl.when(jnp.logical_not(want))
        def _():
            buf[...] = jnp.zeros_like(buf)

        return lambda c: links.wait(buf.at[pl.ds(c * size, size)], got + c, want)

    def send_state(k):
        e = 1 if k == levels else 1 << k
        return later_start(A.at[k], LA.at[k], e, q >= e, q + e < groups, PARTS[k])

    def send_map(k, half):
        e = 1 << k
        return later_start(HF.at[k, half, mine] if k else H0.at[half], LH.at[k, :, pl.ds(half * h, h)], e,
                           jnp.logical_and(q >= e, q + e < groups), q + 2 * e < groups, 1)

    gather1.end()
    gather3 = Gather(GF.at[3], False).start()
    rows1.receive()
    turn_a = turn_of(dot(DR[0], GF[0]))
    whole_product(HA, GF.at[1], GF.at[0])()
    turn = turn_of(dot(SB[0], HA[...]))
    for half in (0, 1):
        H0[half] = dot(Hb, HA[:, half * h:half * h + h]).astype(BF16)
    got_h = [send_map(0, half) for half in (0, 1)] if levels > 1 else []
    turn_a.receive()
    Sa = (column(0) + dot(turn_a.turned(), GF[0])).astype(BF16)
    gather3.mid()
    turn.receive()
    A[0] = (Sa.astype(F32) + dot(turn.turned(), HA[...])).astype(BF16)
    got_a = send_state(0)
    own = turn_of(A[0])
    turn_c = turn_of(dot(SB[0], GF[1]))
    turn_s = turn_of(SB[0])
    gather3.end()
    got_hb = whole_product(HB, GF.at[3], GF.at[2])
    sent, got = links.take(), links.take()
    for j in range(4):
        at = rows(4 * i + j)
        for half in (0, 1):
            HF[0, half, at] = dot(HB[at], HA[:, half * h:half * h + h]).astype(BF16)
        links.copy(HF.at[0, :, at], HF.at[0, :, at], sent, got, sib, x)
    links.later(HF.at[0, :, my_rows], sent)
    links.wait(HF.at[0, :, its_rows], got)
    gathers = []
    def small(a, b, dims):
        return lax.dot_general(a, b, (dims, ((), ())), precision=lax.Precision.HIGHEST,
                               preferred_element_type=F32)

    def by_lanes(a, b):
        return lax.dot_general(a, b, (((1,), (1,)), ((), ())), preferred_element_type=F32)

    ar = R.shape[1]
    maps = {3: GF.at[3], 2: HB, 1: HC}
    ready = {}

    def prepare(k):
        if k == max(levels - 2, 0):
            got_hb()
            ready["hc"] = whole_product(HC, HB, GF.at[1])
        if k == levels - 1:
            ready["hc"]()
            turn_c.receive()
            SB[1] = (column(1) + dot(turn_c.turned(), GF[1])).astype(BF16)
            turn_s.receive()
            ready["own"] = {3: DC[3].T, 2: turn_s.turned(), 1: SB[1]}
            lanes = [RR[t, :, pl.ds(pl.multiple_of(me * m, m), m)].astype(F32)
                     for t in range(4)]
            ready["lanes"] = lanes[0]
            ready["total"] = sum(
                small(by_lanes(ready["own"][t], RR[t]), lanes[t], ((0,), (1,)))
                for t in (1, 2, 3))
            ready["V"] = {t: by_lanes(RR[t], maps[t][mine]) for t in (1, 2, 3)}

    for k in range(levels):
        final = k + 1 == levels
        ends, gathers, got = gathers, [], []
        def compose(half):
            HF[k + 1, half, mine] = dot(LH[k], HF[k, half]).astype(BF16)
            gathers.append(Gather(HF.at[k + 1, half]).start())
            if k + 2 < levels:
                got.append(send_map(k + 1, half))

        def apply():
            size = m // PARTS[k]
            for c in range(PARTS[k]):
                got_a(c)
                for half in (0, 1):
                    turn.send(c, dot(LA[k, pl.ds(c * size, size)], HF[k, half]), half)

        turn = new_turn(PARTS[k])
        if k == 0:
            apply()
            if not final:
                for received in got_h:
                    received(0)
                compose(0)
                compose(1)
        else:
            ends[0].end()
            if not final:
                for received in got_h:
                    received(0)
                compose(0)
            ends[1].end()
            if k not in FIRST and not final:
                compose(1)
            if k + 1 >= levels - 1:
                prepare(k)
            apply()
            if k in FIRST and not final:
                compose(1)
        got_h = got
        if not final:
            gathers[0].mid()
        if k + 2 == levels:
            gathers[1].mid()
        own.receive()
        before = own.turned().astype(F32)
        turn.receive()
        columns = turn.turned()
        for half in (0, 1):
            at = pl.ds(half * h, h)
            A[k + 1, :, at] = (before[:, half * h:half * h + h]
                               + dot(columns, HF[k, half])).astype(BF16)
        got_a = send_state(k + 1)
        if not final:
            own = turn_of(A[k + 1])
            if k + 2 != levels:
                gathers[1].mid()

    class RowsOut:
        def __init__(self, src, core, s):
            self.core, self.s, self.got = core, s, links.take()
            to, sent, near = sig.at[s, mine], links.take(), links.take()
            for d in (1, 3, 2):
                links.copy(src.at[:, panel(around[d])], to, sent, self.got, 2 * q + core, around[d])
            links.copy(src.at[:, panel(x)], to, near, self.got, sib, x, i != core)
            links.keep(src.at[:, panel(x)], to, self.got, i == core)
            links.later(src.at[:, pl.ds(0, 3 * w)], sent)
            links.later(src.at[:, panel(x)], near, i != core)

        def receive(self):
            links.wait(sig.at[self.s], self.got, i == self.core)

    class ColumnsOut:
        def __init__(self, stage, value, core, s):
            self.core, self.s, self.got, sent = core, s, links.take(), links.take()
            stage[...] = value.T
            links.copy(stage, sig.at[s, :, my_lanes], sent, self.got, sib, x, i != core)
            links.later(stage, sent, i != core)

            @pl.when(i == core)
            def _():
                sig[s, :, my_lanes] = stage[...]

        def receive(self):
            links.wait(sig.at[self.s, :, its_lanes], self.got, i == self.core)

    class Sum:
        def __init__(self, buf, place, value, others):
            size = buf.shape[0]
            self.buf, self.others, sent, self.got = (
                buf, buf.at[pl.ds(0, size - 1)], links.take(), links.take())
            buf[place] = value
            for device in others:
                links.copy(buf.at[place], buf.at[place], sent, self.got, *device)
            links.later(self.others, sent)

        def receive(self):
            links.wait(self.others, self.got)
            out = self.buf[0]
            for k in range(1, self.buf.shape[0]):
                out += self.buf[k]
            return out

    if levels == 1:
        prepare(0)
    out0 = RowsOut(A.at[levels], 0, 0)
    own_terms, V = ready["own"], ready["V"]
    total = ready["total"] + small(ready["lanes"], by_lanes(A[levels], RR[0]), ((1,), (0,)))
    turns_out = {t: new_turn(PARTS[levels]) for t in (3, 2, 1)}
    lm = m // PARTS[levels]
    for c in range(PARTS[levels]):
        at = pl.ds(c * lm, lm)
        got_a(c)
        products = {}
        for t in (3, 2, 1):
            products[t] = dot(LA[levels, at], maps[t][...]).astype(BF16)
            if c + 1 < PARTS[levels]:
                turns_out[t].send(c, products[t])
        for t in (1, 2, 3):
            total += small(V[t][:, c * lm:c * lm + lm], by_lanes(products[t], RR[t]),
                           ((1,), (0,)))
    total = jnp.concatenate([total, jnp.zeros((ar, C1.shape[2] - ar), F32)], axis=1)
    corner_sum = Sum(C1, me, total, [(sib, x)] + [(2 * q + c, chip) for chip, c in ring])
    for t in (3, 2, 1):
        turns_out[t].send(PARTS[levels] - 1, products[t])

    def sigma_of(t):
        turns_out[t].receive()
        value = (own_terms[t].astype(F32) + dot(turns_out[t].turned(), maps[t][...])).astype(BF16)
        return ColumnsOut(OT.at[t - 1], value, t // 2, t % 2)

    outs = [out0]
    total = corner_sum.receive()
    if gy > 1:
        corner_sum = Sum(C2, qy, total, [(2 * g + i, x) for g in ys])
    outs += [sigma_of(3), sigma_of(2)]
    if gy > 1:
        total = corner_sum.receive()
    if gz > 1:
        corner_sum = Sum(C3, qz, total, [(2 * g + i, x) for g in zs])
    outs.append(sigma_of(1))
    for out in outs:
        out.receive()
    for s in (0, 1):
        arrow[s] = dot(RR[2 * i + s], sig[s]).astype(BF16)
    if gz > 1:
        total = corner_sum.receive()
    corner[...] = cb[...] + total[:, :ar] / (4 * groups)
    links.later(PS.at[pl.ds(0, turns[0]), pl.ds(0, 2 * X - 1)], t_sent)
    links.drain()


def passed_on(*refs):
    count = len(refs) // 2
    for src, dst in zip(refs[:count], refs[count:]):
        dst[...] = src[...]


def shards(precision_blocks, coupling, arrow_rows, corner_base):
    groups = lax.axis_size("tm") // 2
    levels = groups.bit_length() - 1
    assert levels % 2 == 1
    n, w = precision_blocks.shape[1:]
    ar = arrow_rows.shape[1]
    h, m = n // 2, w // 2
    vmem = pl.BlockSpec(memory_space=pltpu.VMEM)
    far = pl.BlockSpec(memory_space=pl.ANY)
    turns = 2 * levels + 8
    shapes = (
        jax.ShapeDtypeStruct(precision_blocks.shape, BF16),
        jax.ShapeDtypeStruct((2, ar, w), BF16),
        jax.ShapeDtypeStruct((ar, ar), F32),
    )
    results = pl.pallas_call(
        functools.partial(kernel, groups),
        out_shape=shapes,
        in_specs=[far, far, far, vmem],
        out_specs=(vmem,) * 3,
        scratch_shapes=[
            pltpu.VMEM((4, n, n), BF16),
            pltpu.VMEM((n, n), BF16),
            pltpu.VMEM((n, n), BF16),
            pltpu.VMEM((n, n), BF16),
            pltpu.VMEM((2, m, n // 2), BF16),
            pltpu.VMEM((levels, 2, n, h), BF16),
            pltpu.VMEM((levels + 1, m, n), BF16),
            pltpu.VMEM((levels + 1, m, n), BF16),
            pltpu.VMEM((levels, m, n), BF16),
            pltpu.VMEM((turns, 2 * X, m, m), BF16),
            pltpu.VMEM((turns, n, m), BF16),
            pltpu.VMEM((4, n, m), BF16),
            pltpu.VMEM((2, m, n), BF16),
            pltpu.VMEM((2, m, n), BF16),
            pltpu.VMEM((4, ar, n), BF16),
            pltpu.VMEM((3, n, m), BF16),
            pltpu.VMEM((8, ar, 128), F32),
            pltpu.VMEM((min(4, groups), ar, 128), F32),
            pltpu.VMEM((max(1, groups // 4), ar, 128), F32),
            pltpu.SemaphoreType.DMA((SEMS,)),
        ],
        compiler_params=pltpu.CompilerParams(
            collective_id=0, has_side_effects=True, vmem_limit_bytes=60 * 1024 * 1024),
        cost_estimate=pl.CostEstimate(
            flops=2 * 22 * w * n * n, bytes_accessed=4 << 20, transcendentals=0),
    )(precision_blocks, coupling, arrow_rows, corner_base)
    return pl.pallas_call(
        passed_on,
        out_shape=shapes,
        in_specs=[vmem] * 3,
        out_specs=(vmem,) * 3,
    )(*results)


def solution(mesh):
    return jax.shard_map(
        shards,
        mesh=mesh,
        in_specs=(P("tm", None, "col"), P("tm", "col", None), P("tm", None, None), P()),
        out_specs=(P("tm", None, "col"), P("tm", None, "col"), P()),
        check_vma=False,
    )
```
